32 devices in a mesh: fsdp: 32 (over z, y, x, core).
Axes of the slice: x: 2, y: 2, z: 4, core: 2. Of those that a mesh axis runs over, the one named last changes fastest.
Arguments:
- tokens: bfloat16 [16384, 896], P('fsdp'), may hold values from -6 to 6
- lengths: int32 [48], replicated, may hold values from 1 to 512, 16384 in all
- gains: bfloat16 [1792], P('fsdp'), may hold values from 0.5 to 1.5
- w_qkv: bfloat16 [1032192], P('fsdp'), may hold values from -0.1875 to 0.1875
- b_qkv: bfloat16 [1152], P('fsdp'), may hold values from -3 to 3
- w_out: bfloat16 [802816], P('fsdp'), may hold values from -0.75 to 0.75
- w_gate_up: bfloat16 [8716288], P('fsdp'), may hold values from -0.1875 to 0.1875
- w_down: bfloat16 [4358144], P('fsdp'), may hold values from -0.078125 to 0.078125
- grad_out: bfloat16 [16384, 896], P('fsdp'), may hold values from -6 to 6
Outputs:
- output: bfloat16 [16384, 896], P('fsdp')
- grad_tokens: float32 [16384, 896], P('fsdp')
- grad_gains: float32 [1792], P('fsdp')
- grad_w_qkv: float32 [1032192], P('fsdp')
- grad_b_qkv: float32 [1152], P('fsdp')
- grad_w_out: float32 [802816], P('fsdp')
- grad_w_gate_up: float32 [8716288], P('fsdp')
- grad_w_down: float32 [4358144], P('fsdp')
The draws below stay inside these ranges and needn't reach their ends.
Inputs may be any that keep to these rules, and one draw needn't show every extreme that they name: Sequences lie end to end in order; the lengths sum to 16384 and the longest has exactly 512 tokens.
All inputs are finite; a program needn't handle non-finite values.
Results may differ from the reference program's by a relative error of at most 0.011.
Values may be sent and summed in bfloat16 or wider, within the bound.
A program may use at most 256 MiB of HBM per device.

```python
import math
import jax
import jax.numpy as jnp
import numpy as np
from jax import lax

D = 896
FF = 4864
HEADS = 14
KV_HEADS = 2
HD = 64
TOK_DEV = 512
MOST = 512
QKV = 1152
TOKENS = 16384
SEQS = 48
BIAS_LEN = 1152


def levels(own_key, extent, cuts, smallest, largest):
    factor_of, own = 1.0, jax.random.fold_in(own_key, 6)
    for dim, shards_of in cuts:
        steps = jnp.exp(jax.random.uniform(jax.random.fold_in(own, dim), (shards_of,), jnp.float32, smallest / len(cuts), largest / len(cuts)))
        factor_of = factor_of * jnp.repeat(steps, extent[dim] // shards_of).reshape([-1 if axis == dim else 1 for axis in range(len(extent))])
    return factor_of


def length_profile(amount, total, limit, lean):
    weights = [(1 << 20) // math.isqrt(grade ** lean) + 1 for grade in range(2, amount + 1)]
    spare, holding = total - limit - (amount - 1), [1] * (amount - 1)
    while spare > 0:
        candidates = [i for i in range(amount - 1) if holding[i] < limit]
        whole, remaining = sum([weights[i] for i in candidates]), spare
        for i in candidates:
            more = min(limit - holding[i], max(1, remaining * weights[i] // whole), spare)
            holding[i] = holding[i] + more
            spare = spare - more
    return np.array([limit] + holding)


def ragged(stream_key, amount, total, reach, skew):
    if amount == 2:
        one = jax.random.randint(stream_key, (), max(1, total - reach), min(reach, total - 1) + 1)
        return jnp.stack([one, total - one])
    sizes = jnp.asarray(length_profile(amount, total, reach, skew), jnp.int32)
    pairs = (amount - 1) // 2
    source_of, taker = sizes[1:1 + 2 * pairs:2], sizes[2:2 + 2 * pairs:2]
    room = jnp.minimum(source_of - 1, reach - taker)
    moved = jax.random.randint(jax.random.fold_in(stream_key, 1), (pairs,), 0, 1 << 20) % (room + 1)
    sizes = sizes.at[1:1 + 2 * pairs:2].set(source_of - moved).at[2:2 + 2 * pairs:2].set(taker + moved)
    return sizes[jax.random.permutation(jax.random.fold_in(stream_key, 2), amount)]


def normal_values(stream_key, shape, width, limit, shards=(), kind=jnp.bfloat16):
    entries = jax.random.normal(stream_key, shape, jnp.float32) * width
    if len(shards) > 0:
        entries = levels(stream_key, shape, shards, -0.22, 0.18) * entries
    return jnp.clip(entries, min=-limit, max=limit).astype(kind)


def setup_inputs(seed: int = 0) -> dict:
    key_list = jax.random.split(jax.random.key(seed), 10)
    return {
        "tokens": normal_values(key_list[0], (TOKENS, D), 1.0, 6.0, ((0, 32),)),
        "lengths": ragged(key_list[1], SEQS, TOKENS, MOST, 0).astype(jnp.int32),
        "gains": jnp.clip(1.0 + 0.1 * jax.random.normal(key_list[2], (2 * D,), jnp.float32), 0.5, 1.5).astype(jnp.bfloat16),
        "w_qkv": normal_values(key_list[3], (D * QKV,), D ** -0.5, 0.1875, ((0, 32),)),
        "b_qkv": normal_values(key_list[4], (BIAS_LEN,), 0.5, 3.0, ((0, 32),)),
        "w_out": normal_values(key_list[5], (HEADS * HD * D,), (D // 16) ** -0.5, 0.75, ((0, 32),)),
        "w_gate_up": normal_values(key_list[6], (2 * D * FF,), D ** -0.5, 0.1875, ((0, 32),)),
        "w_down": normal_values(key_list[7], (FF * D,), FF ** -0.5, 0.078125, ((0, 32),)),
        "grad_out": normal_values(key_list[8], (TOKENS, D), 1.0, 6.0, ((0, 32),)),
    }


EPSILON = 1e-06
ROPE_BASE = 1000000.0
MASKED_SCORE = -1e+30

@jax.custom_vjp
def low(v):
    return lax.optimization_barrier(v.astype(jnp.bfloat16)).astype(jnp.float32)

@jax.custom_vjp
def low_back(v):
    return v

def low_keep(v):
    return (low(v), None)

def low_pass(kept, grad):
    return (grad,)

def back_keep(v):
    return (v, None)

def back_low(kept, grad):
    return (low(grad),)
low.defvjp(low_keep, low_pass)
low_back.defvjp(back_keep, back_low)

def matmul_hi(left, right):
    return jnp.dot(left, right, precision=lax.Precision.HIGHEST)

def rms_norm(hidden, gain):
    factor = lax.rsqrt(lax.optimization_barrier(jnp.mean(hidden * hidden, axis=1, keepdims=True)) + EPSILON)
    return hidden * factor * gain

def rope_tables(positions, head_dim):
    half_dim = head_dim // 2
    frequency = ROPE_BASE ** (-(2.0 * jnp.arange(half_dim, dtype=jnp.float32)) / head_dim)
    angles = positions.astype(jnp.float32)[:, None] * frequency[None, :]
    angles = jnp.concatenate([angles, angles], axis=1)
    return (jnp.cos(angles)[:, None, :], jnp.sin(angles)[:, None, :])

def rotate(values, cosine, sine):
    half_dim = values.shape[-1] // 2
    turned = jnp.concatenate([-values[..., half_dim:], values[..., :half_dim]], axis=-1)
    return values * cosine + turned * sine

def reference(tokens, lengths, gains, w_qkv, b_qkv, w_out, w_gate_up, w_down, grad_out):
    block_rows = min(4 * TOK_DEV, 2048)
    blocks = TOKENS // block_rows
    query_dim = HEADS * HD
    kv_dim = KV_HEADS * HD
    groups = HEADS // KV_HEADS
    scale = 1.0 / math.sqrt(HD)
    token_index = jnp.arange(TOKENS, dtype=jnp.int32)
    ends = jnp.cumsum(lengths, dtype=jnp.int32)
    before = ends[None, :] <= token_index[:, None]
    segment = lax.optimization_barrier(jnp.sum(before.astype(jnp.int32), axis=1, dtype=jnp.int32))
    position = token_index - lax.optimization_barrier(jnp.sum(jnp.where(before, lengths[None, :], 0), axis=1, dtype=jnp.int32))
    seg_pad = jnp.concatenate([jnp.full((MOST,), -1, jnp.int32), segment])
    index_pad = jnp.arange(-MOST, TOKENS, dtype=jnp.int32)

    def forward(hidden, gains_f, wqkv_f, bias_f, wout_f, wgu_f, wdown_f):
        gain_one = gains_f[:D]
        gain_two = gains_f[D:]
        wqkv = wqkv_f.reshape(D, QKV)
        wout = wout_f.reshape(query_dim, D)
        wgu = wgu_f.reshape(D, 2 * FF)
        wdown = wdown_f.reshape(FF, D)

        def project(pair):
            rows_in, rows_pos = pair
            normed = low(rms_norm(rows_in, gain_one))
            linear = low_back(matmul_hi(normed, wqkv) + bias_f[:QKV])
            cosine, sine = rope_tables(rows_pos, HD)
            query = linear[:, :query_dim].reshape(-1, HEADS, HD)
            keyed = linear[:, query_dim:query_dim + kv_dim].reshape(-1, KV_HEADS, HD)
            query = low(rotate(query, cosine, sine)).reshape(-1, query_dim)
            keyed = low(rotate(keyed, cosine, sine)).reshape(-1, kv_dim)
            valued = low(linear[:, query_dim + kv_dim:])
            return (query, keyed, valued)
        hidden_blocks = hidden.reshape(blocks, block_rows, D)
        query, keyed, valued = lax.map(jax.checkpoint(project), (hidden_blocks, position.reshape(blocks, block_rows)))
        query = query.reshape(TOKENS, query_dim)
        key_pad = jnp.concatenate([jnp.zeros((MOST, kv_dim), keyed.dtype), keyed.reshape(TOKENS, kv_dim)])
        value_pad = jnp.concatenate([jnp.zeros((MOST, kv_dim), valued.dtype), valued.reshape(TOKENS, kv_dim)])

        def attend(number):
            offset = (number * block_rows).astype(jnp.int32)
            rows_q = lax.dynamic_slice_in_dim(query, offset, block_rows).reshape(block_rows, KV_HEADS, groups, HD)
            key_block = lax.dynamic_slice_in_dim(key_pad, offset, block_rows + MOST).reshape(-1, KV_HEADS, HD)
            value_block = lax.dynamic_slice_in_dim(value_pad, offset, block_rows + MOST).reshape(-1, KV_HEADS, HD)
            query_seg = lax.dynamic_slice_in_dim(segment, offset, block_rows)
            query_idx = lax.dynamic_slice_in_dim(token_index, offset, block_rows)
            key_seg = lax.dynamic_slice_in_dim(seg_pad, offset, block_rows + MOST)
            key_idx = lax.dynamic_slice_in_dim(index_pad, offset, block_rows + MOST)
            allowed = (key_seg[None, :] == query_seg[:, None]) & (key_idx[None, :] <= query_idx[:, None]) & (key_idx[None, :] >= 0)
            scores = low_back(jnp.einsum('qkgd,jkd->kgqj', rows_q, key_block, precision=lax.Precision.HIGHEST) * scale)
            scores = jnp.where(allowed[None, None], scores, MASKED_SCORE)
            probs = low(jax.nn.softmax(scores, axis=-1))
            mixed = jnp.einsum('kgqj,jkd->qkgd', probs, value_block, precision=lax.Precision.HIGHEST)
            return low(low_back(mixed.reshape(block_rows, query_dim)))
        attended = lax.map(jax.checkpoint(attend), jnp.arange(blocks, dtype=jnp.int32))

        def finish(pair):
            rows_in, rows_att = pair
            middle = rows_in + low_back(matmul_hi(rows_att, wout))
            normed = low(rms_norm(middle, gain_two))
            gate_up = low_back(matmul_hi(normed, wgu))
            product = low(jax.nn.silu(gate_up[:, :FF]) * gate_up[:, FF:])
            return middle + low_back(matmul_hi(product, wdown))
        result = lax.map(jax.checkpoint(finish), (hidden_blocks, attended))
        return result.reshape(TOKENS, D)
    primals = (tokens.astype(jnp.float32), gains.astype(jnp.float32), w_qkv.astype(jnp.float32), b_qkv.astype(jnp.float32), w_out.astype(jnp.float32), w_gate_up.astype(jnp.float32), w_down.astype(jnp.float32))
    result, pullback = jax.vjp(forward, *primals)
    grads = pullback(grad_out.astype(jnp.float32))
    return (result.astype(jnp.bfloat16), grads[0], grads[1], grads[2], grads[3], grads[4], grads[5], grads[6])
```

```python
import math

import jax
import jax.numpy as jnp
from jax import lax
from jax.sharding import PartitionSpec as P

FF = 4864
HEADS = 14
KV_HEADS = 2
HD = 64
QKV = 1152


EPSILON = 1e-06
ROPE_BASE = 1000000.0
MASKED_SCORE = -1e30


def passed_along(x, axis, by):
    peers = lax.axis_size(axis)
    pairs = [(i, i + by) for i in range(peers) if 0 <= i + by < peers]
    return lax.ppermute(x, axis, pairs)


def rope_tables(positions, head_dim):
    half_dim = head_dim // 2
    frequency = ROPE_BASE ** (-(2.0 * jnp.arange(half_dim, dtype=jnp.float32)) / head_dim)
    angles = positions.astype(jnp.float32)[:, None] * frequency[None, :]
    angles = jnp.concatenate([angles, angles], axis=1)
    return (jnp.cos(angles)[:, None, :], jnp.sin(angles)[:, None, :])


def turn_half(values):
    half_dim = values.shape[-1] // 2
    return jnp.concatenate([-values[..., half_dim:], values[..., :half_dim]], axis=-1)


def rotate(values, cosine, sine):
    return values * cosine + turn_half(values) * sine


def unrotate(values, cosine, sine):
    return values * cosine - turn_half(values) * sine


def segment_info(lengths, base_index, count):
    token_index = base_index + jnp.arange(count, dtype=jnp.int32)
    ends = jnp.cumsum(lengths, dtype=jnp.int32)
    before = ends[None, :] <= token_index[:, None]
    segment = jnp.sum(before.astype(jnp.int32), axis=1, dtype=jnp.int32)
    start_of = jnp.sum(jnp.where(before, lengths[None, :], 0), axis=1, dtype=jnp.int32)
    return (token_index, segment, token_index - start_of)


def outer_sum(left, right):
    return lax.dot_general(
        left, right, (((0,), (0,)), ((), ())), preferred_element_type=jnp.float32
    )


def back_dot(left, right):
    return lax.dot_general(
        left, right, (((1,), (1,)), ((), ())), preferred_element_type=jnp.float32
    )


def unpack_attention(params, width):
    full_gains, qkv_flat, bias_flat, out_flat = params
    return (
        full_gains[:width].astype(jnp.float32),
        full_gains[width:].astype(jnp.float32),
        qkv_flat.reshape(width, QKV),
        bias_flat[:QKV].astype(jnp.float32),
        out_flat.reshape(HEADS * HD, width),
    )


def unpack_mlp(params, width):
    gu_flat, down_flat = params
    return (gu_flat.reshape(width, 2 * FF), down_flat.reshape(FF, width))


def partner_swap(x, bit):
    peers = lax.axis_size("fsdp")
    return lax.ppermute(x, "fsdp", [(i, i ^ (1 << bit)) for i in range(peers)])


def my_bit(bit):
    return (lax.axis_index("fsdp") >> bit) & 1


def halve(x, axis, bit):
    mine = my_bit(bit)
    sent = lax.dynamic_index_in_dim(x, 1 - mine, axis, keepdims=False).astype(jnp.bfloat16)
    kept = lax.dynamic_index_in_dim(x, mine, axis, keepdims=False)
    return kept.astype(jnp.float32) + partner_swap(sent, bit).astype(jnp.float32)


def reduce_to_owner(x, bits, order):
    left = list(bits)
    x = x.reshape((2,) * len(left) + x.shape[1:])
    for bit in order:
        x = halve(x, left.index(bit), bit)
        left.remove(bit)
        if left:
            x = x.astype(jnp.bfloat16)
    return x


def norm_back(grad_normed, hidden, factor, gain):
    normed = hidden * factor
    grad_gain = jnp.sum(grad_normed * normed, axis=0)
    scaled = grad_normed * gain
    grad_hidden = factor * scaled - normed * factor * jnp.mean(
        scaled * normed, axis=1, keepdims=True
    )
    return (grad_hidden, grad_gain)


def local(tokens, lengths, gains, w_qkv, b_qkv, w_out, w_gate_up, w_down, grad_out):
    tok_rows = tokens.shape[0]
    width = tokens.shape[1]
    n_devices = lax.axis_size("fsdp")
    query_dim = HEADS * HD
    kv_dim = KV_HEADS * HD
    groups = HEADS // KV_HEADS
    scale = 1.0 / math.sqrt(HD)
    block_rows = min(tok_rows, 512)
    block_count = tok_rows // block_rows
    rows_own = width // n_devices
    core = my_bit(0)
    chips = n_devices // 2
    attn_sizes = (w_qkv.shape[0], w_out.shape[0], gains.shape[0], b_qkv.shape[0])
    attn_flat = jnp.concatenate([w_qkv, w_out, gains, b_qkv])
    attn_flat = jnp.pad(attn_flat, (0, -attn_flat.shape[0] % 1024))
    attn_all = lax.all_gather(attn_flat, "fsdp", axis=0, tiled=True).reshape(n_devices, -1)
    pieces, at = [], 0
    for size in attn_sizes:
        pieces.append(attn_all[:, at : at + size].reshape(-1))
        at += size
    gain_one, gain_two, wqkv, bias, wout = unpack_attention(
        (pieces[2], pieces[0], pieces[3], pieces[1]), width
    )
    whole_rows = width % n_devices == 0
    if whole_rows:
        gu_own = w_gate_up.reshape(rows_own, 2, FF)
        gu_own = (gu_own[:, 0], gu_own[:, 1])
        gu_kept = jnp.where(core == 0, gu_own[0], gu_own[1])
        gu_came = partner_swap(jnp.where(core == 0, gu_own[1], gu_own[0]), 0)
        gu_chip = jnp.where(
            core == 0,
            jnp.concatenate([gu_kept, gu_came]),
            jnp.concatenate([gu_came, gu_kept]),
        )
        gu_chip, attn_all = lax.optimization_barrier((gu_chip, attn_all))
        gu_all = lax.all_gather(gu_chip, "fsdp", axis=0, tiled=True)
        gu_all = gu_all.reshape(chips, 2, 2 * rows_own, FF)
        wgate = gu_all[:, 0].reshape(width, FF)
        wup = gu_all[:, 1].reshape(width, FF)
    else:
        gu_all = lax.all_gather(w_gate_up, "fsdp", axis=0, tiled=True).reshape(width, 2 * FF)
        wgate, wup = gu_all[:, :FF], gu_all[:, FF:]
    down_own, gu_all = lax.optimization_barrier((w_down.reshape(FF // n_devices, width), gu_all))
    wdown = lax.all_gather(down_own, "fsdp", axis=0, tiled=True)
    base_index = lax.axis_index("fsdp") * tok_rows
    token_index, segment, position = segment_info(lengths, base_index, tok_rows)
    prev_index, prev_segment, unused_pos = segment_info(lengths, base_index - tok_rows, tok_rows)
    key_index = jnp.concatenate([prev_index, token_index])
    key_segment = jnp.concatenate([prev_segment, segment])
    hidden = tokens.astype(jnp.float32)
    factor_one = lax.rsqrt(jnp.mean(hidden * hidden, axis=1, keepdims=True) + EPSILON)
    normed_one = (hidden * factor_one * gain_one).astype(jnp.bfloat16)
    linear = jnp.dot(normed_one, wqkv, preferred_element_type=jnp.float32) + bias
    cosine, sine = rope_tables(position, HD)
    query = rotate(linear[:, :query_dim].reshape(tok_rows, HEADS, HD), cosine, sine).astype(
        jnp.bfloat16
    )
    keyed = rotate(
        linear[:, query_dim : query_dim + kv_dim].reshape(tok_rows, KV_HEADS, HD), cosine, sine
    )
    keyed = keyed.astype(jnp.bfloat16).reshape(tok_rows, kv_dim)
    valued = linear[:, query_dim + kv_dim :].astype(jnp.bfloat16)
    key_prev, value_prev = passed_along((keyed, valued), "fsdp", 1)
    key_all = jnp.concatenate([key_prev, keyed]).reshape(2 * tok_rows, KV_HEADS, HD)
    value_all = jnp.concatenate([value_prev, valued]).reshape(2 * tok_rows, KV_HEADS, HD)
    query_four = query.reshape(tok_rows, KV_HEADS, groups, HD)

    def scores_of():
        allowed = (
            (key_segment[None, :] == segment[:, None])
            & (key_index[None, :] <= token_index[:, None])
            & (key_index[None, :] >= 0)
        )
        scores = (
            jnp.einsum("qkgd,jkd->kgqj", query_four, key_all, preferred_element_type=jnp.float32)
            * scale
        )
        scores = jnp.where(allowed[None, None], scores, MASKED_SCORE)
        return (query_four, key_all, value_all, scores)

    def attend(number):
        rows_q, key_block, value_block, scores = scores_of()
        row_max = jnp.max(scores, axis=-1, keepdims=True)
        weight = jnp.exp(scores - row_max)
        row_sum = jnp.sum(weight, axis=-1, keepdims=True)
        probs = (weight / row_sum).astype(jnp.bfloat16)
        mixed = jnp.einsum("kgqj,jkd->qkgd", probs, value_block, preferred_element_type=jnp.float32)
        return (mixed.reshape(block_rows, query_dim), row_max + jnp.log(row_sum))

    mixed_blocks, log_sums = lax.map(attend, jnp.arange(block_count, dtype=jnp.int32))
    attended = mixed_blocks.reshape(tok_rows, query_dim).astype(jnp.bfloat16)
    middle = hidden + jnp.dot(attended, wout, preferred_element_type=jnp.float32)
    factor_two = lax.rsqrt(jnp.mean(middle * middle, axis=1, keepdims=True) + EPSILON)
    normed_two = (middle * factor_two * gain_two).astype(jnp.bfloat16)
    gate_pre = jnp.dot(normed_two, wgate, preferred_element_type=jnp.float32)
    up_pre = jnp.dot(normed_two, wup, preferred_element_type=jnp.float32)
    sigma = jax.nn.sigmoid(gate_pre)
    silu_gate = gate_pre * sigma
    product = (silu_gate * up_pre).astype(jnp.bfloat16)
    output = (middle + jnp.dot(product, wdown, preferred_element_type=jnp.float32)).astype(
        jnp.bfloat16
    )
    bits = tuple(range(n_devices.bit_length() - 2, -1, -1))
    far = bits[: len(bits) - 4]
    grad_down = outer_sum(product, grad_out).astype(jnp.bfloat16)
    down_parts = halve(grad_down.reshape(chips, 2, -1, width), 1, 0).astype(jnp.bfloat16)
    down_sum = reduce_to_owner(down_parts, bits[:-1], (3, 1, 2) + far)
    grad_product = back_dot(grad_out, wdown)
    grad_gate = grad_product * up_pre * sigma * (1.0 + gate_pre * (1.0 - sigma))
    grad_up = grad_product * silu_gate
    grad_gate = grad_gate.astype(jnp.bfloat16)
    grad_up = grad_up.astype(jnp.bfloat16)
    if whole_rows:
        gu_sent = outer_sum(normed_two, jnp.where(core == 0, grad_up, grad_gate))
        gu_came = partner_swap(gu_sent.astype(jnp.bfloat16), 0)
        gu_kept = outer_sum(normed_two, jnp.where(core == 0, grad_gate, grad_up))
        gu_parts = (gu_kept + gu_came.astype(jnp.float32)).astype(jnp.bfloat16)
        gu_parts = gu_parts.reshape(chips, 2 * rows_own, FF)
        gu_sums = (
            reduce_to_owner(gu_parts[:, :, : FF // 2], bits[:-1], (1, 2, 3) + far),
            reduce_to_owner(gu_parts[:, :, FF // 2 :], bits[:-1], (2, 3, 1) + far),
        )
        gu_sum = jnp.concatenate(gu_sums, axis=1).reshape(2, rows_own, FF)
        gu_kept = lax.dynamic_index_in_dim(gu_sum, core, 0, keepdims=False)
        gu_came = partner_swap(lax.dynamic_index_in_dim(gu_sum, 1 - core, 0, keepdims=False), 0)
        grad_wgu = jnp.concatenate(
            [jnp.where(core == 0, gu_kept, gu_came), jnp.where(core == 0, gu_came, gu_kept)], axis=1
        )
    else:
        grad_gu = jnp.concatenate([grad_gate, grad_up], axis=1)
        gu_parts = outer_sum(normed_two, grad_gu).astype(jnp.bfloat16)
        grad_wgu = reduce_to_owner(gu_parts.reshape(n_devices, -1), bits, (0, 1, 2, 3) + far)
    grad_normed_two = back_dot(grad_gate, wgate) + back_dot(grad_up, wup)
    grad_middle_norm, grad_gain_two = norm_back(grad_normed_two, middle, factor_two, gain_two)
    grad_middle = grad_out.astype(jnp.float32) + grad_middle_norm
    grad_branch = grad_middle.astype(jnp.bfloat16)
    grad_wout = outer_sum(attended, grad_branch).astype(jnp.bfloat16)
    wout_sum = reduce_to_owner(
        grad_wout.reshape((n_devices, -1, width) if whole_rows else (n_devices, -1)),
        bits,
        (0, 2, 3, 1) + far,
    )
    grad_att = back_dot(grad_branch, wout).astype(jnp.bfloat16)
    grad_att_four = grad_att.reshape(tok_rows, KV_HEADS, groups, HD)

    def back_block(number, carried):
        grad_query, grad_key, grad_value = carried
        rows_q, key_block, value_block, scores = scores_of()
        probs = jnp.exp(scores - log_sums[number])
        grad_probs = jnp.einsum(
            "qkgd,jkd->kgqj", grad_att_four, value_block, preferred_element_type=jnp.float32
        )
        inner = jnp.sum(probs * grad_probs, axis=-1, keepdims=True)
        grad_scores = (probs * (grad_probs - inner)).astype(jnp.bfloat16)
        part_query = (
            jnp.einsum("kgqj,jkd->qkgd", grad_scores, key_block, preferred_element_type=jnp.float32)
            * scale
        )
        part_key = (
            jnp.einsum("kgqj,qkgd->jkd", grad_scores, rows_q, preferred_element_type=jnp.float32)
            * scale
        )
        part_value = jnp.einsum(
            "kgqj,qkgd->jkd",
            probs.astype(jnp.bfloat16),
            grad_att_four,
            preferred_element_type=jnp.float32,
        )
        grad_query = part_query
        grad_key = grad_key + part_key
        grad_value = grad_value + part_value
        return (grad_query, grad_key, grad_value)

    start_state = (
        jnp.zeros((tok_rows, KV_HEADS, groups, HD), jnp.float32),
        jnp.zeros((2 * tok_rows, KV_HEADS, HD), jnp.float32),
        jnp.zeros((2 * tok_rows, KV_HEADS, HD), jnp.float32),
    )
    grad_query, grad_key, grad_value = lax.fori_loop(0, block_count, back_block, start_state)
    key_back, value_back = (
        passed_along(grad_key[:tok_rows].astype(jnp.bfloat16), "fsdp", -1).astype(jnp.float32),
        passed_along(grad_value[:tok_rows].astype(jnp.bfloat16), "fsdp", -1).astype(jnp.float32),
    )
    grad_key_own = grad_key[tok_rows:] + key_back
    grad_value_own = (grad_value[tok_rows:] + value_back).reshape(tok_rows, kv_dim)
    grad_query_lin = unrotate(grad_query.reshape(tok_rows, HEADS, HD), cosine, sine).reshape(
        tok_rows, query_dim
    )
    grad_key_lin = unrotate(grad_key_own, cosine, sine).reshape(tok_rows, kv_dim)
    grad_linear = jnp.concatenate([grad_query_lin, grad_key_lin, grad_value_own], axis=1).astype(
        jnp.bfloat16
    )
    grad_wqkv = outer_sum(normed_one, grad_linear)
    grad_bias = jnp.sum(grad_linear.astype(jnp.float32), axis=0)
    grad_normed_one = back_dot(grad_linear, wqkv)
    grad_hidden_norm, grad_gain_one = norm_back(grad_normed_one, hidden, factor_one, gain_one)
    grad_tokens = grad_middle + grad_hidden_norm
    gains_own, bias_own = gains.shape[0], b_qkv.shape[0]
    grad_bias_full = jnp.pad(grad_bias, (0, bias_own * n_devices - QKV))
    grad_gains_full = jnp.concatenate([grad_gain_one, grad_gain_two])
    vectors = jnp.concatenate(
        [grad_gains_full.reshape(n_devices, -1), grad_bias_full.reshape(n_devices, -1)], axis=1
    )
    if whole_rows:
        vectors = jnp.pad(vectors, ((0, 0), (0, QKV - vectors.shape[1])))[:, None]
        grad_wqkv = grad_wqkv.reshape(n_devices, rows_own, QKV)
    else:
        grad_wqkv = grad_wqkv.reshape(n_devices, -1)
    last = jnp.concatenate([grad_wqkv, vectors], axis=1).astype(jnp.bfloat16)
    last_sum = reduce_to_owner(last, bits, (0, 1, 2, 3) + far).reshape(-1)
    qkv_own = w_qkv.shape[0]
    return (
        output,
        grad_tokens,
        last_sum[qkv_own : qkv_own + gains_own],
        last_sum[:qkv_own],
        last_sum[qkv_own + gains_own : qkv_own + gains_own + bias_own],
        wout_sum.reshape(-1),
        grad_wgu.reshape(-1),
        down_sum.reshape(-1),
    )


def solution(mesh):
    in_specs = (
        P("fsdp", None),
        P(),
        P("fsdp"),
        P("fsdp"),
        P("fsdp"),
        P("fsdp"),
        P("fsdp"),
        P("fsdp"),
        P("fsdp", None),
    )
    out_specs = (
        P("fsdp", None),
        P("fsdp", None),
        P("fsdp"),
        P("fsdp"),
        P("fsdp"),
        P("fsdp"),
        P("fsdp"),
        P("fsdp"),
    )
    return jax.shard_map(local, mesh=mesh, in_specs=in_specs, out_specs=out_specs, check_vma=False)
```

```python
import math

import jax
import jax.numpy as jnp
from jax import lax
from jax.sharding import PartitionSpec as P

FF = 4864
HEADS = 14
KV_HEADS = 2
HD = 64
QKV = 1152


EPSILON = 1e-06
ROPE_BASE = 1000000.0
MASKED_SCORE = -1e30


def passed_along(x, axis, by):
    peers = lax.axis_size(axis)
    pairs = [(i, i + by) for i in range(peers) if 0 <= i + by < peers]
    return lax.ppermute(x, axis, pairs)


def rope_tables(positions, head_dim):
    half_dim = head_dim // 2
    frequency = ROPE_BASE ** (-(2.0 * jnp.arange(half_dim, dtype=jnp.float32)) / head_dim)
    angles = positions.astype(jnp.float32)[:, None] * frequency[None, :]
    angles = jnp.concatenate([angles, angles], axis=1)
    return (jnp.cos(angles)[:, None, :], jnp.sin(angles)[:, None, :])


def turn_half(values):
    half_dim = values.shape[-1] // 2
    return jnp.concatenate([-values[..., half_dim:], values[..., :half_dim]], axis=-1)


def rotate(values, cosine, sine):
    return values * cosine + turn_half(values) * sine


def unrotate(values, cosine, sine):
    return values * cosine - turn_half(values) * sine


def segment_info(lengths, base_index, count):
    token_index = base_index + jnp.arange(count, dtype=jnp.int32)
    ends = jnp.cumsum(lengths, dtype=jnp.int32)
    before = ends[None, :] <= token_index[:, None]
    segment = jnp.sum(before.astype(jnp.int32), axis=1, dtype=jnp.int32)
    start_of = jnp.sum(jnp.where(before, lengths[None, :], 0), axis=1, dtype=jnp.int32)
    return (token_index, segment, token_index - start_of)


def outer_sum(left, right):
    return lax.dot_general(
        left, right, (((0,), (0,)), ((), ())), preferred_element_type=jnp.float32
    )


def back_dot(left, right):
    return lax.dot_general(
        left, right, (((1,), (1,)), ((), ())), preferred_element_type=jnp.float32
    )


def unpack_attention(params, width):
    full_gains, qkv_flat, bias_flat, out_flat = params
    return (
        full_gains[:width].astype(jnp.float32),
        full_gains[width:].astype(jnp.float32),
        qkv_flat.reshape(width, QKV),
        bias_flat[:QKV].astype(jnp.float32),
        out_flat.reshape(HEADS * HD, width),
    )


def unpack_mlp(params, width):
    gu_flat, down_flat = params
    return (gu_flat.reshape(width, 2 * FF), down_flat.reshape(FF, width))


def partner_swap(x, bit):
    peers = lax.axis_size("fsdp")
    return lax.ppermute(x, "fsdp", [(i, i ^ (1 << bit)) for i in range(peers)])


def my_bit(bit):
    return (lax.axis_index("fsdp") >> bit) & 1


def halve(x, axis, bit):
    mine = my_bit(bit)
    sent = lax.dynamic_index_in_dim(x, 1 - mine, axis, keepdims=False).astype(jnp.bfloat16)
    kept = lax.dynamic_index_in_dim(x, mine, axis, keepdims=False)
    return kept.astype(jnp.float32) + partner_swap(sent, bit).astype(jnp.float32)


def reduce_step(x, bits, order, upto):
    left = list(bits)
    x = x.reshape((2,) * len(left) + x.shape[1:])
    for bit in order[:upto]:
        x = halve(x, left.index(bit), bit)
        left.remove(bit)
        if left:
            x = x.astype(jnp.bfloat16)
    x = x.reshape((-1,) + x.shape[len(left) :]) if left else x
    return (x, tuple(left), tuple(order[upto:]))


def reduce_to_owner(x, bits, order):
    return reduce_step(x, bits, order, len(order))[0]


def norm_back(grad_normed, hidden, factor, gain):
    normed = hidden * factor
    grad_gain = jnp.sum(grad_normed * normed, axis=0)
    scaled = grad_normed * gain
    grad_hidden = factor * scaled - normed * factor * jnp.mean(
        scaled * normed, axis=1, keepdims=True
    )
    return (grad_hidden, grad_gain)


def local(tokens, lengths, gains, w_qkv, b_qkv, w_out, w_gate_up, w_down, grad_out):
    tok_rows = tokens.shape[0]
    width = tokens.shape[1]
    n_devices = lax.axis_size("fsdp")
    query_dim = HEADS * HD
    kv_dim = KV_HEADS * HD
    groups = HEADS // KV_HEADS
    scale = 1.0 / math.sqrt(HD)
    block_rows = min(tok_rows, 512)
    block_count = tok_rows // block_rows
    rows_own = width // n_devices
    core = my_bit(0)
    chips = n_devices // 2
    attn_sizes = (w_qkv.shape[0], w_out.shape[0], gains.shape[0], b_qkv.shape[0])
    attn_flat = jnp.concatenate([w_qkv, w_out, gains, b_qkv])
    attn_flat = jnp.pad(attn_flat, (0, -attn_flat.shape[0] % 1024))
    attn_all = lax.all_gather(attn_flat, "fsdp", axis=0, tiled=True).reshape(n_devices, -1)
    pieces, at = [], 0
    for size in attn_sizes:
        pieces.append(attn_all[:, at : at + size].reshape(-1))
        at += size
    gain_one, gain_two, wqkv, bias, wout = unpack_attention(
        (pieces[2], pieces[0], pieces[3], pieces[1]), width
    )
    whole_rows = width % n_devices == 0
    if whole_rows:
        gu_own = w_gate_up.reshape(rows_own, 2, FF)
        gu_own = (gu_own[:, 0], gu_own[:, 1])
        gu_kept = jnp.where(core == 0, gu_own[0], gu_own[1])
        gu_came = partner_swap(jnp.where(core == 0, gu_own[1], gu_own[0]), 0)
        gu_chip = jnp.where(
            core == 0,
            jnp.concatenate([gu_kept, gu_came]),
            jnp.concatenate([gu_came, gu_kept]),
        )
        gu_chip, attn_all = lax.optimization_barrier((gu_chip, attn_all))
        gu_all = lax.all_gather(gu_chip, "fsdp", axis=0, tiled=True)
        gu_all = gu_all.reshape(chips, 2, 2 * rows_own, FF)
        wgate = gu_all[:, 0].reshape(width, FF)
        wup = gu_all[:, 1].reshape(width, FF)
    else:
        gu_all = lax.all_gather(w_gate_up, "fsdp", axis=0, tiled=True).reshape(width, 2 * FF)
        wgate, wup = gu_all[:, :FF], gu_all[:, FF:]
    base_index = lax.axis_index("fsdp") * tok_rows
    token_index, segment, position = segment_info(lengths, base_index, tok_rows)
    prev_index, prev_segment, unused_pos = segment_info(lengths, base_index - tok_rows, tok_rows)
    key_index = jnp.concatenate([prev_index, token_index])
    key_segment = jnp.concatenate([prev_segment, segment])
    hidden = tokens.astype(jnp.float32)
    factor_one = lax.rsqrt(jnp.mean(hidden * hidden, axis=1, keepdims=True) + EPSILON)
    normed_one = (hidden * factor_one * gain_one).astype(jnp.bfloat16)
    linear = jnp.dot(normed_one, wqkv, preferred_element_type=jnp.float32) + bias
    cosine, sine = rope_tables(position, HD)
    query = rotate(linear[:, :query_dim].reshape(tok_rows, HEADS, HD), cosine, sine).astype(
        jnp.bfloat16
    )
    keyed = rotate(
        linear[:, query_dim : query_dim + kv_dim].reshape(tok_rows, KV_HEADS, HD), cosine, sine
    )
    keyed = keyed.astype(jnp.bfloat16).reshape(tok_rows, kv_dim)
    valued = linear[:, query_dim + kv_dim :].astype(jnp.bfloat16)
    down_own, keyed = lax.optimization_barrier((w_down.reshape(FF // n_devices, width), keyed))
    wdown = lax.all_gather(down_own, "fsdp", axis=0, tiled=True)
    key_prev, value_prev = passed_along((keyed, valued), "fsdp", 1)
    key_all = jnp.concatenate([key_prev, keyed]).reshape(2 * tok_rows, KV_HEADS, HD)
    value_all = jnp.concatenate([value_prev, valued]).reshape(2 * tok_rows, KV_HEADS, HD)
    query_four = query.reshape(tok_rows, KV_HEADS, groups, HD)

    def scores_of():
        allowed = (
            (key_segment[None, :] == segment[:, None])
            & (key_index[None, :] <= token_index[:, None])
            & (key_index[None, :] >= 0)
        )
        scores = (
            jnp.einsum("qkgd,jkd->kgqj", query_four, key_all, preferred_element_type=jnp.float32)
            * scale
        )
        scores = jnp.where(allowed[None, None], scores, MASKED_SCORE)
        return (query_four, key_all, value_all, scores)

    def attend(number):
        rows_q, key_block, value_block, scores = scores_of()
        row_max = jnp.max(scores, axis=-1, keepdims=True)
        weight = jnp.exp(scores - row_max)
        row_sum = jnp.sum(weight, axis=-1, keepdims=True)
        probs = (weight / row_sum).astype(jnp.bfloat16)
        mixed = jnp.einsum("kgqj,jkd->qkgd", probs, value_block, preferred_element_type=jnp.float32)
        return (mixed.reshape(block_rows, query_dim), row_max + jnp.log(row_sum))

    mixed_blocks, log_sums = lax.map(attend, jnp.arange(block_count, dtype=jnp.int32))
    attended = mixed_blocks.reshape(tok_rows, query_dim).astype(jnp.bfloat16)
    middle = hidden + jnp.dot(attended, wout, preferred_element_type=jnp.float32)
    factor_two = lax.rsqrt(jnp.mean(middle * middle, axis=1, keepdims=True) + EPSILON)
    normed_two = (middle * factor_two * gain_two).astype(jnp.bfloat16)
    gate_pre = jnp.dot(normed_two, wgate, preferred_element_type=jnp.float32)
    up_pre = jnp.dot(normed_two, wup, preferred_element_type=jnp.float32)
    sigma = jax.nn.sigmoid(gate_pre)
    silu_gate = gate_pre * sigma
    product = (silu_gate * up_pre).astype(jnp.bfloat16)
    output = (middle + jnp.dot(product, wdown, preferred_element_type=jnp.float32)).astype(
        jnp.bfloat16
    )
    bits = tuple(range(n_devices.bit_length() - 2, -1, -1))
    far = bits[: len(bits) - 4]
    grad_down = outer_sum(product, grad_out).astype(jnp.bfloat16)
    down_parts = halve(grad_down.reshape(chips, 2, -1, width), 1, 0).astype(jnp.bfloat16)
    grad_product = back_dot(grad_out, wdown)
    grad_gate = grad_product * up_pre * sigma * (1.0 + gate_pre * (1.0 - sigma))
    grad_up = grad_product * silu_gate
    grad_gate = grad_gate.astype(jnp.bfloat16)
    grad_up = grad_up.astype(jnp.bfloat16)
    chip_bits = bits[:-1]
    moving = [(down_parts, chip_bits, (3, 1, 2) + far)]
    if whole_rows:
        gu_sent = outer_sum(normed_two, jnp.where(core == 0, grad_up, grad_gate))
        gu_came = partner_swap(gu_sent.astype(jnp.bfloat16), 0)
        gu_kept = outer_sum(normed_two, jnp.where(core == 0, grad_gate, grad_up))
        gu_kept = gu_kept.astype(jnp.bfloat16)
    else:
        grad_gu = jnp.concatenate([grad_gate, grad_up], axis=1)
        gu_parts = outer_sum(normed_two, grad_gu).astype(jnp.bfloat16)
        moving.append((gu_parts.reshape(n_devices, -1), bits, (0, 1, 2, 3) + far))
    grad_normed_two = back_dot(grad_gate, wgate) + back_dot(grad_up, wup)
    grad_middle_norm, grad_gain_two = norm_back(grad_normed_two, middle, factor_two, gain_two)
    grad_middle = grad_out.astype(jnp.float32) + grad_middle_norm
    grad_branch = grad_middle.astype(jnp.bfloat16)
    if whole_rows:
        grad_branch, gu_kept, gu_came, down_parts = lax.optimization_barrier(
            (grad_branch, gu_kept, gu_came, down_parts)
        )
        gu_parts = (gu_kept.astype(jnp.float32) + gu_came.astype(jnp.float32)).astype(jnp.bfloat16)
        gu_parts = gu_parts.reshape(chips, 2 * rows_own, FF)
        moving = [
            (down_parts, chip_bits, (3, 1, 2) + far),
            (gu_parts[:, :, : FF // 2], chip_bits, (1, 2, 3) + far),
            (gu_parts[:, :, FF // 2 :], chip_bits, (2, 3, 1) + far),
        ]
    grad_wout = outer_sum(attended, grad_branch).astype(jnp.bfloat16)
    grad_wout = grad_wout.reshape((n_devices, -1, width) if whole_rows else (n_devices, -1))
    moving.append((grad_wout, bits, (0, 2, 3, 1) + far))

    def one_step(moving, held):
        stepped = [reduce_step(*part, 1) for part in moving]
        held, sums = lax.optimization_barrier((held, [part[0] for part in stepped]))
        return ([(x,) + part[1:] for x, part in zip(sums, stepped)], held)

    grad_att = back_dot(grad_branch, wout).astype(jnp.bfloat16)
    grad_att_four = grad_att.reshape(tok_rows, KV_HEADS, groups, HD)

    rows_q, key_block, value_block, scores = scores_of()
    probs = jnp.exp(scores - log_sums[0])
    grad_probs = jnp.einsum(
        "qkgd,jkd->kgqj", grad_att_four, value_block, preferred_element_type=jnp.float32
    )
    inner = jnp.sum(probs * grad_probs, axis=-1, keepdims=True)
    moving, inner = one_step(moving, inner)
    grad_scores = (probs * (grad_probs - inner)).astype(jnp.bfloat16)
    grad_key = (
        jnp.einsum("kgqj,qkgd->jkd", grad_scores, rows_q, preferred_element_type=jnp.float32)
        * scale
    )
    grad_value = jnp.einsum(
        "kgqj,qkgd->jkd",
        probs.astype(jnp.bfloat16),
        grad_att_four,
        preferred_element_type=jnp.float32,
    )
    grad_query = (
        jnp.einsum("kgqj,jkd->qkgd", grad_scores, key_block, preferred_element_type=jnp.float32)
        * scale
    )
    key_back, value_back = (
        passed_along(grad_key[:tok_rows].astype(jnp.bfloat16), "fsdp", -1).astype(jnp.float32),
        passed_along(grad_value[:tok_rows].astype(jnp.bfloat16), "fsdp", -1).astype(jnp.float32),
    )
    grad_key_own = grad_key[tok_rows:] + key_back
    grad_value_own = (grad_value[tok_rows:] + value_back).reshape(tok_rows, kv_dim)
    grad_query_lin = unrotate(grad_query.reshape(tok_rows, HEADS, HD), cosine, sine).reshape(
        tok_rows, query_dim
    )
    grad_key_lin = unrotate(grad_key_own, cosine, sine).reshape(tok_rows, kv_dim)
    grad_linear = jnp.concatenate([grad_query_lin, grad_key_lin, grad_value_own], axis=1).astype(
        jnp.bfloat16
    )
    moving, grad_linear = one_step(moving, grad_linear)
    grad_wqkv = outer_sum(normed_one, grad_linear)
    grad_bias = jnp.sum(grad_linear.astype(jnp.float32), axis=0)
    grad_normed_one = back_dot(grad_linear, wqkv)
    grad_hidden_norm, grad_gain_one = norm_back(grad_normed_one, hidden, factor_one, gain_one)
    grad_tokens = grad_middle + grad_hidden_norm
    gains_own, bias_own = gains.shape[0], b_qkv.shape[0]
    grad_bias_full = jnp.pad(grad_bias, (0, bias_own * n_devices - QKV))
    grad_gains_full = jnp.concatenate([grad_gain_one, grad_gain_two])
    vectors = jnp.concatenate(
        [grad_gains_full.reshape(n_devices, -1), grad_bias_full.reshape(n_devices, -1)], axis=1
    )
    if whole_rows:
        vectors = jnp.pad(vectors, ((0, 0), (0, QKV - vectors.shape[1])))[:, None]
        grad_wqkv = grad_wqkv.reshape(n_devices, rows_own, QKV)
    else:
        grad_wqkv = grad_wqkv.reshape(n_devices, -1)
    last = jnp.concatenate([grad_wqkv, vectors], axis=1).astype(jnp.bfloat16)
    last_sum = reduce_to_owner(last, bits, (0, 1, 2, 3) + far).reshape(-1)
    qkv_own = w_qkv.shape[0]
    sums = [reduce_to_owner(*part) for part in moving]
    down_sum, wout_sum = sums[0], sums[-1]
    if whole_rows:
        gu_sum = jnp.concatenate(sums[1:3], axis=1).reshape(2, rows_own, FF)
        gu_kept = lax.dynamic_index_in_dim(gu_sum, core, 0, keepdims=False)
        gu_came = partner_swap(lax.dynamic_index_in_dim(gu_sum, 1 - core, 0, keepdims=False), 0)
        grad_wgu = jnp.concatenate(
            [jnp.where(core == 0, gu_kept, gu_came), jnp.where(core == 0, gu_came, gu_kept)],
            axis=1,
        )
    else:
        grad_wgu = sums[1]
    return (
        output,
        grad_tokens,
        last_sum[qkv_own : qkv_own + gains_own],
        last_sum[:qkv_own],
        last_sum[qkv_own + gains_own : qkv_own + gains_own + bias_own],
        wout_sum.reshape(-1),
        grad_wgu.reshape(-1),
        down_sum.reshape(-1),
    )


def solution(mesh):
    in_specs = (
        P("fsdp", None),
        P(),
        P("fsdp"),
        P("fsdp"),
        P("fsdp"),
        P("fsdp"),
        P("fsdp"),
        P("fsdp"),
        P("fsdp", None),
    )
    out_specs = (
        P("fsdp", None),
        P("fsdp", None),
        P("fsdp"),
        P("fsdp"),
        P("fsdp"),
        P("fsdp"),
        P("fsdp"),
        P("fsdp"),
    )
    return jax.shard_map(local, mesh=mesh, in_specs=in_specs, out_specs=out_specs, check_vma=False)
```

```python
import math

import jax
import jax.numpy as jnp
from jax import lax
from jax.sharding import PartitionSpec as P

FF = 4864
HEADS = 14
KV_HEADS = 2
HD = 64
QKV = 1152


EPSILON = 1e-06
ROPE_BASE = 1000000.0
MASKED_SCORE = -1e30


def passed_along(x, axis, by):
    peers = lax.axis_size(axis)
    pairs = [(i, i + by) for i in range(peers) if 0 <= i + by < peers]
    return lax.ppermute(x, axis, pairs)


def rope_tables(positions, head_dim):
    half_dim = head_dim // 2
    frequency = ROPE_BASE ** (-(2.0 * jnp.arange(half_dim, dtype=jnp.float32)) / head_dim)
    angles = positions.astype(jnp.float32)[:, None] * frequency[None, :]
    angles = jnp.concatenate([angles, angles], axis=1)
    return (jnp.cos(angles)[:, None, :], jnp.sin(angles)[:, None, :])


def turn_half(values):
    half_dim = values.shape[-1] // 2
    return jnp.concatenate([-values[..., half_dim:], values[..., :half_dim]], axis=-1)


def rotate(values, cosine, sine):
    return values * cosine + turn_half(values) * sine


def unrotate(values, cosine, sine):
    return values * cosine - turn_half(values) * sine


def segment_info(lengths, base_index, count):
    token_index = base_index + jnp.arange(count, dtype=jnp.int32)
    ends = jnp.cumsum(lengths, dtype=jnp.int32)
    before = ends[None, :] <= token_index[:, None]
    segment = jnp.sum(before.astype(jnp.int32), axis=1, dtype=jnp.int32)
    start_of = jnp.sum(jnp.where(before, lengths[None, :], 0), axis=1, dtype=jnp.int32)
    return (token_index, segment, token_index - start_of)


def outer_sum(left, right):
    return lax.dot_general(
        left, right, (((0,), (0,)), ((), ())), preferred_element_type=jnp.float32
    )


def back_dot(left, right):
    return lax.dot_general(
        left, right, (((1,), (1,)), ((), ())), preferred_element_type=jnp.float32
    )


def unpack_attention(params, width):
    full_gains, qkv_flat, bias_flat, out_flat = params
    return (
        full_gains[:width].astype(jnp.float32),
        full_gains[width:].astype(jnp.float32),
        qkv_flat.reshape(width, QKV),
        bias_flat[:QKV].astype(jnp.float32),
        out_flat.reshape(HEADS * HD, width),
    )


def unpack_mlp(params, width):
    gu_flat, down_flat = params
    return (gu_flat.reshape(width, 2 * FF), down_flat.reshape(FF, width))


def partner_swap(x, bit):
    peers = lax.axis_size("fsdp")
    return lax.ppermute(x, "fsdp", [(i, i ^ (1 << bit)) for i in range(peers)])


def my_bit(bit):
    return (lax.axis_index("fsdp") >> bit) & 1


def halve(x, axis, bit):
    mine = my_bit(bit)
    sent = lax.dynamic_index_in_dim(x, 1 - mine, axis, keepdims=False).astype(jnp.bfloat16)
    kept = lax.dynamic_index_in_dim(x, mine, axis, keepdims=False)
    return kept.astype(jnp.float32) + partner_swap(sent, bit).astype(jnp.float32)


def reduce_step(x, bits, order, upto):
    left = list(bits)
    x = x.reshape((2,) * len(left) + x.shape[1:])
    for bit in order[:upto]:
        x = halve(x, left.index(bit), bit)
        left.remove(bit)
        if left:
            x = x.astype(jnp.bfloat16)
    x = x.reshape((-1,) + x.shape[len(left) :]) if left else x
    return (x, tuple(left), tuple(order[upto:]))


def reduce_to_owner(x, bits, order):
    return reduce_step(x, bits, order, len(order))[0] if order else x


def norm_back(grad_normed, hidden, factor, gain):
    normed = hidden * factor
    grad_gain = jnp.sum(grad_normed * normed, axis=0)
    scaled = grad_normed * gain
    grad_hidden = factor * scaled - normed * factor * jnp.mean(
        scaled * normed, axis=1, keepdims=True
    )
    return (grad_hidden, grad_gain)


def local(tokens, lengths, gains, w_qkv, b_qkv, w_out, w_gate_up, w_down, grad_out):
    tok_rows = tokens.shape[0]
    width = tokens.shape[1]
    n_devices = lax.axis_size("fsdp")
    query_dim = HEADS * HD
    kv_dim = KV_HEADS * HD
    groups = HEADS // KV_HEADS
    scale = 1.0 / math.sqrt(HD)
    block_rows = min(tok_rows, 512)
    block_count = tok_rows // block_rows
    rows_own = width // n_devices
    core = my_bit(0)
    chips = n_devices // 2
    attn_sizes = (w_qkv.shape[0], w_out.shape[0], gains.shape[0], b_qkv.shape[0])
    attn_flat = jnp.concatenate([w_qkv, w_out, gains, b_qkv])
    attn_flat = jnp.pad(attn_flat, (0, -attn_flat.shape[0] % 1024))
    attn_all = lax.all_gather(attn_flat, "fsdp", axis=0, tiled=True).reshape(n_devices, -1)
    pieces, at = [], 0
    for size in attn_sizes:
        pieces.append(attn_all[:, at : at + size].reshape(-1))
        at += size
    gain_one, gain_two, wqkv, bias, wout = unpack_attention(
        (pieces[2], pieces[0], pieces[3], pieces[1]), width
    )
    whole_rows = width % n_devices == 0
    if whole_rows:
        gu_own = w_gate_up.reshape(rows_own, 2, FF)
        gu_own = (gu_own[:, 0], gu_own[:, 1])
        gu_kept = jnp.where(core == 0, gu_own[0], gu_own[1])
        gu_came = partner_swap(jnp.where(core == 0, gu_own[1], gu_own[0]), 0)
        gu_chip = jnp.where(
            core == 0,
            jnp.concatenate([gu_kept, gu_came]),
            jnp.concatenate([gu_came, gu_kept]),
        )
        gu_chip, attn_all = lax.optimization_barrier((gu_chip, attn_all))
        gu_all = lax.all_gather(gu_chip, "fsdp", axis=0, tiled=True)
        gu_all = gu_all.reshape(chips, 2, 2 * rows_own, FF)
        wgate = gu_all[:, 0].reshape(width, FF)
        wup = gu_all[:, 1].reshape(width, FF)
    else:
        gu_all = lax.all_gather(w_gate_up, "fsdp", axis=0, tiled=True).reshape(width, 2 * FF)
        wgate, wup = gu_all[:, :FF], gu_all[:, FF:]
    base_index = lax.axis_index("fsdp") * tok_rows
    token_index, segment, position = segment_info(lengths, base_index, tok_rows)
    prev_index, prev_segment, unused_pos = segment_info(lengths, base_index - tok_rows, tok_rows)
    key_index = jnp.concatenate([prev_index, token_index])
    key_segment = jnp.concatenate([prev_segment, segment])
    hidden = tokens.astype(jnp.float32)
    factor_one = lax.rsqrt(jnp.mean(hidden * hidden, axis=1, keepdims=True) + EPSILON)
    normed_one = (hidden * factor_one * gain_one).astype(jnp.bfloat16)
    linear = jnp.dot(normed_one, wqkv, preferred_element_type=jnp.float32) + bias
    cosine, sine = rope_tables(position, HD)
    query = rotate(linear[:, :query_dim].reshape(tok_rows, HEADS, HD), cosine, sine).astype(
        jnp.bfloat16
    )
    keyed = rotate(
        linear[:, query_dim : query_dim + kv_dim].reshape(tok_rows, KV_HEADS, HD), cosine, sine
    )
    keyed = keyed.astype(jnp.bfloat16).reshape(tok_rows, kv_dim)
    valued = linear[:, query_dim + kv_dim :].astype(jnp.bfloat16)
    down_own, keyed = lax.optimization_barrier((w_down.reshape(FF // n_devices, width), keyed))
    wdown = lax.all_gather(down_own, "fsdp", axis=0, tiled=True)
    key_prev, value_prev = passed_along((keyed, valued), "fsdp", 1)
    key_all = jnp.concatenate([key_prev, keyed]).reshape(2 * tok_rows, KV_HEADS, HD)
    value_all = jnp.concatenate([value_prev, valued]).reshape(2 * tok_rows, KV_HEADS, HD)
    query_four = query.reshape(tok_rows, KV_HEADS, groups, HD)

    def scores_of():
        allowed = (
            (key_segment[None, :] == segment[:, None])
            & (key_index[None, :] <= token_index[:, None])
            & (key_index[None, :] >= 0)
        )
        scores = (
            jnp.einsum("qkgd,jkd->kgqj", query_four, key_all, preferred_element_type=jnp.float32)
            * scale
        )
        scores = jnp.where(allowed[None, None], scores, MASKED_SCORE)
        return (query_four, key_all, value_all, scores)

    def attend(number):
        rows_q, key_block, value_block, scores = scores_of()
        row_max = jnp.max(scores, axis=-1, keepdims=True)
        weight = jnp.exp(scores - row_max)
        row_sum = jnp.sum(weight, axis=-1, keepdims=True)
        probs = (weight / row_sum).astype(jnp.bfloat16)
        mixed = jnp.einsum("kgqj,jkd->qkgd", probs, value_block, preferred_element_type=jnp.float32)
        return (mixed.reshape(block_rows, query_dim), row_max + jnp.log(row_sum))

    mixed_blocks, log_sums = lax.map(attend, jnp.arange(block_count, dtype=jnp.int32))
    attended = mixed_blocks.reshape(tok_rows, query_dim).astype(jnp.bfloat16)
    middle = hidden + jnp.dot(attended, wout, preferred_element_type=jnp.float32)
    factor_two = lax.rsqrt(jnp.mean(middle * middle, axis=1, keepdims=True) + EPSILON)
    normed_two = (middle * factor_two * gain_two).astype(jnp.bfloat16)
    gate_pre = jnp.dot(normed_two, wgate, preferred_element_type=jnp.float32)
    up_pre = jnp.dot(normed_two, wup, preferred_element_type=jnp.float32)
    sigma = jax.nn.sigmoid(gate_pre)
    silu_gate = gate_pre * sigma
    product = (silu_gate * up_pre).astype(jnp.bfloat16)
    output = (middle + jnp.dot(product, wdown, preferred_element_type=jnp.float32)).astype(
        jnp.bfloat16
    )
    bits = tuple(range(n_devices.bit_length() - 2, -1, -1))
    far = bits[: len(bits) - 4]
    grad_down = outer_sum(product, grad_out).astype(jnp.bfloat16)
    down_parts = halve(grad_down.reshape(chips, 2, -1, width), 1, 0).astype(jnp.bfloat16)
    grad_product = back_dot(grad_out, wdown)
    grad_gate = grad_product * up_pre * sigma * (1.0 + gate_pre * (1.0 - sigma))
    grad_up = grad_product * silu_gate
    grad_gate = grad_gate.astype(jnp.bfloat16)
    grad_up = grad_up.astype(jnp.bfloat16)
    chip_bits = bits[:-1]
    moving = [(down_parts, chip_bits, (3, 1, 2) + far)]
    if whole_rows:
        gu_sent = outer_sum(normed_two, jnp.where(core == 0, grad_up, grad_gate))
        gu_came = partner_swap(gu_sent.astype(jnp.bfloat16), 0)
        gu_kept = outer_sum(normed_two, jnp.where(core == 0, grad_gate, grad_up))
        gu_kept = gu_kept.astype(jnp.bfloat16)
    else:
        grad_gu = jnp.concatenate([grad_gate, grad_up], axis=1)
        gu_parts = outer_sum(normed_two, grad_gu).astype(jnp.bfloat16)
        moving.append((gu_parts.reshape(n_devices, -1), bits, (0, 1, 2, 3) + far))
    grad_normed_two = back_dot(grad_gate, wgate) + back_dot(grad_up, wup)
    grad_middle_norm, grad_gain_two = norm_back(grad_normed_two, middle, factor_two, gain_two)
    grad_middle = grad_out.astype(jnp.float32) + grad_middle_norm
    grad_branch = grad_middle.astype(jnp.bfloat16)
    if whole_rows:
        grad_branch, gu_kept, gu_came, down_parts = lax.optimization_barrier(
            (grad_branch, gu_kept, gu_came, down_parts)
        )
        gu_parts = (gu_kept.astype(jnp.float32) + gu_came.astype(jnp.float32)).astype(jnp.bfloat16)
        gu_parts = gu_parts.reshape(chips, 2 * rows_own, FF)
        moving = [
            (down_parts, chip_bits, (3, 1, 2) + far),
            (gu_parts[:, :, : FF // 2], chip_bits, (1, 2, 3) + far),
            (gu_parts[:, :, FF // 2 :], chip_bits, (2, 3, 1) + far),
        ]
    grad_wout = outer_sum(attended, grad_branch).astype(jnp.bfloat16)
    grad_wout = grad_wout.reshape((n_devices, -1, width) if whole_rows else (n_devices, -1))
    moving.append((grad_wout, bits, (0, 2, 3, 1) + far))

    def one_step(moving, held):
        stepped = [reduce_step(*part, 1) for part in moving]
        held, sums = lax.optimization_barrier((held, [part[0] for part in stepped]))
        return ([(x,) + part[1:] for x, part in zip(sums, stepped)], held)

    grad_att = back_dot(grad_branch, wout).astype(jnp.bfloat16)
    grad_att_four = grad_att.reshape(tok_rows, KV_HEADS, groups, HD)

    rows_q, key_block, value_block, scores = scores_of()
    probs = jnp.exp(scores - log_sums[0])
    grad_probs = jnp.einsum(
        "qkgd,jkd->kgqj", grad_att_four, value_block, preferred_element_type=jnp.float32
    )
    inner = jnp.sum(probs * grad_probs, axis=-1, keepdims=True)
    moving, inner = one_step(moving, inner)
    grad_scores = (probs * (grad_probs - inner)).astype(jnp.bfloat16)
    moving, grad_scores = one_step(moving, grad_scores)
    grad_key = (
        jnp.einsum("kgqj,qkgd->jkd", grad_scores, rows_q, preferred_element_type=jnp.float32)
        * scale
    )
    grad_value = jnp.einsum(
        "kgqj,qkgd->jkd",
        probs.astype(jnp.bfloat16),
        grad_att_four,
        preferred_element_type=jnp.float32,
    )
    grad_query = (
        jnp.einsum("kgqj,jkd->qkgd", grad_scores, key_block, preferred_element_type=jnp.float32)
        * scale
    )
    key_back, value_back = (
        passed_along(grad_key[:tok_rows].astype(jnp.bfloat16), "fsdp", -1).astype(jnp.float32),
        passed_along(grad_value[:tok_rows].astype(jnp.bfloat16), "fsdp", -1).astype(jnp.float32),
    )
    grad_key_own = grad_key[tok_rows:] + key_back
    grad_value_own = (grad_value[tok_rows:] + value_back).reshape(tok_rows, kv_dim)
    grad_query_lin = unrotate(grad_query.reshape(tok_rows, HEADS, HD), cosine, sine).reshape(
        tok_rows, query_dim
    )
    grad_key_lin = unrotate(grad_key_own, cosine, sine).reshape(tok_rows, kv_dim)
    grad_linear = jnp.concatenate([grad_query_lin, grad_key_lin, grad_value_own], axis=1).astype(
        jnp.bfloat16
    )
    moving, grad_linear = one_step(moving, grad_linear)
    grad_wqkv = outer_sum(normed_one, grad_linear)
    grad_bias = jnp.sum(grad_linear.astype(jnp.float32), axis=0)
    grad_normed_one = back_dot(grad_linear, wqkv)
    grad_hidden_norm, grad_gain_one = norm_back(grad_normed_one, hidden, factor_one, gain_one)
    grad_tokens = grad_middle + grad_hidden_norm
    gains_own, bias_own = gains.shape[0], b_qkv.shape[0]
    grad_bias_full = jnp.pad(grad_bias, (0, bias_own * n_devices - QKV))
    grad_gains_full = jnp.concatenate([grad_gain_one, grad_gain_two])
    vectors = jnp.concatenate(
        [grad_gains_full.reshape(n_devices, -1), grad_bias_full.reshape(n_devices, -1)], axis=1
    )
    if whole_rows:
        vectors = jnp.pad(vectors, ((0, 0), (0, QKV - vectors.shape[1])))[:, None]
        grad_wqkv = grad_wqkv.reshape(n_devices, rows_own, QKV)
    else:
        grad_wqkv = grad_wqkv.reshape(n_devices, -1)
    last = jnp.concatenate([grad_wqkv, vectors], axis=1).astype(jnp.bfloat16)
    last, last_bits, last_order = reduce_step(last, bits, (0, 1, 2, 3) + far, 3)
    moving, last = one_step(moving, last)
    last_sum = reduce_to_owner(last, last_bits, last_order).reshape(-1)
    qkv_own = w_qkv.shape[0]
    sums = [reduce_to_owner(*part) for part in moving]
    down_sum, wout_sum = sums[0], sums[-1]
    if whole_rows:
        gu_sum = jnp.concatenate(sums[1:3], axis=1).reshape(2, rows_own, FF)
        gu_kept = lax.dynamic_index_in_dim(gu_sum, core, 0, keepdims=False)
        gu_came = partner_swap(lax.dynamic_index_in_dim(gu_sum, 1 - core, 0, keepdims=False), 0)
        grad_wgu = jnp.concatenate(
            [jnp.where(core == 0, gu_kept, gu_came), jnp.where(core == 0, gu_came, gu_kept)],
            axis=1,
        )
    else:
        grad_wgu = sums[1]
    return (
        output,
        grad_tokens,
        last_sum[qkv_own : qkv_own + gains_own],
        last_sum[:qkv_own],
        last_sum[qkv_own + gains_own : qkv_own + gains_own + bias_own],
        wout_sum.reshape(-1),
        grad_wgu.reshape(-1),
        down_sum.reshape(-1),
    )


def solution(mesh):
    in_specs = (
        P("fsdp", None),
        P(),
        P("fsdp"),
        P("fsdp"),
        P("fsdp"),
        P("fsdp"),
        P("fsdp"),
        P("fsdp"),
        P("fsdp", None),
    )
    out_specs = (
        P("fsdp", None),
        P("fsdp", None),
        P("fsdp"),
        P("fsdp"),
        P("fsdp"),
        P("fsdp"),
        P("fsdp"),
        P("fsdp"),
    )
    return jax.shard_map(local, mesh=mesh, in_specs=in_specs, out_specs=out_specs, check_vma=False)
```
